32 devices in a mesh: expert: 4 (over y, x), rep: 8 (over z, core).
Axes of the slice: x: 2, y: 2, z: 4, core: 2. Of those that a mesh axis runs over, the one named last changes fastest.
Arguments:
- route_ids: int32 [256, 2], P(('expert', 'rep')), may hold values from 0 to 3, all different within a row; in each aligned block of 8 rows (0 to 7, 8 to 15, ...) at most 4 rows name the same one
- route_weight: float32 [256, 2], P(('expert', 'rep')), may hold values from 0.2 to 0.8
- input_float: bfloat16 [256, 4096], P(('expert', 'rep')), may hold values from -6 to 6
- input_quant: bfloat16 [256, 4096], P(('expert', 'rep')), may hold values from -6 to 6
- keep_mask: int32 [256, 4096], P(('expert', 'rep')), may hold values 0 or 1
- grad_mixed: bfloat16 [256, 4096], P(('expert', 'rep')), may hold values from -192 to 192
- gate_weight: bfloat16 [4, 4096, 7168], P('expert', None, 'rep'), may hold values from -0.09375 to 0.09375
- up_weight: bfloat16 [4, 4096, 7168], P('expert', None, 'rep'), may hold values from -0.09375 to 0.09375
- down_base: bfloat16 [4, 7168, 4096], P('expert', 'rep'), may hold values from -0.0625 to 0.0625
- down_round: bfloat16 [4, 7168, 4096], P('expert', 'rep'), may hold values from -8 to 8
- down_step: float32 [4, 4096], P('expert'), may hold values from 0.004 to 0.04
Outputs:
- mixed: bfloat16 [256, 4096], P(('expert', 'rep'))
- round_grad: float32 [4, 7168, 4096], P('expert', 'rep')
The draws below stay inside these ranges and needn't reach their ends.
Inputs may be any that keep to these rules, and one draw needn't show every extreme that they name: `route_ids`: within the 8 tokens of one device, each expert is named by at most 4 pairs; the two experts of a token differ.
All inputs are finite; a program needn't handle non-finite values. No bound on the sum of `keep_mask` on one device may be relied on, other than what follows from the above.
Results may differ from the reference program's by a relative error of at most 0.0065.
Values may be sent and summed in bfloat16 or wider, within the bound.
A program may use at most 128 MiB of HBM per device.

```python
import math
import jax
import jax.numpy as jnp
import numpy as np
from jax import lax

D = 4096
FF = 7168
TOK_DEV = 8
CAP = 4
EXPERTS = 4
TOKENS = 256


def touch_ends(result, rng, low, top_value):
    index_at = [jax.random.randint(jax.random.fold_in(rng, axis), (), 0, length) for axis, length in enumerate(result.shape)]
    main_axis = result.shape.index(max(result.shape))
    neighbour = index_at[:main_axis] + [(index_at[main_axis] + 1) % result.shape[main_axis]] + index_at[main_axis + 1:]
    return result.at[tuple(index_at)].set(low).at[tuple(neighbour)].set(top_value)


def shard_levels(stream_key, shape, split, low, top_value):
    loudness = 1.0
    for dim, shards_of in split:
        draws = jax.random.uniform(jax.random.fold_in(jax.random.fold_in(stream_key, 6), dim), (shards_of,), jnp.float32, low / len(split), top_value / len(split))
        loudness = loudness * jnp.repeat(jnp.exp(draws), shape[dim] // shards_of).reshape((-1,) + (1,) * (len(shape) - 1 - dim))
    return loudness


def assign_block(own_key, own, number, rows, count, top, limit, slope):
    ranking = jax.random.permutation(own_key, count)
    heavy_load, ordinary = portions_of(count, rows * top, limit, slope, True), portions_of(count, rows * top, limit, slope, False)
    places = jnp.arange(count)

    def named(sizes, offset_by):
        used = int((sizes > 0).sum())
        fixed = max(1, used // 4)
        moved = fixed + (places - fixed + offset_by * (used - fixed)) % max(1, count - fixed)
        return jnp.zeros((count,), jnp.int32).at[ranking[jnp.where(places < fixed, places, moved)]].set(jnp.asarray(sizes, jnp.int32))

    sizes = jnp.where(number % 4 == 0, named(heavy_load, number // 4), named(ordinary, number - number // 4 - 1))
    mixed = jax.random.permutation(jax.random.fold_in(own, 3), count)
    donor, sink = mixed[0:count // 2 * 2:2], mixed[1:count // 2 * 2:2]
    room = jnp.minimum(sizes[donor] - 1, limit - sizes[sink]) // 2
    room = jnp.where((donor == ranking[0]) | (sink == ranking[0]) | (sizes[sink] == 0), 0, jnp.maximum(room, 0))
    moved = jax.random.randint(jax.random.fold_in(own, 4), (count // 2,), 0, 1 << 20) % (room + 1)
    sizes = sizes.at[donor].add(-moved).at[sink].add(moved)
    items = jnp.searchsorted(jnp.cumsum(sizes), jnp.arange(rows * top), side="right").astype(jnp.int32)
    grid = items.reshape(top, rows).T
    grid = grid[jax.random.permutation(jax.random.fold_in(own, 1), rows)]
    offset_by = jax.random.randint(jax.random.fold_in(own, 2), (rows, 1), 0, top)
    return jnp.take_along_axis(grid, (jnp.arange(top)[None, :] + offset_by) % top, axis=1)


def portions_of(count, total, bound, skew, full):
    weights = [(1 << 20) // math.isqrt(standing ** skew) + 1 for standing in range(1, count + 1)]
    largest = bound if full else min(bound, max(-(-total // count), total * weights[0] // sum(weights)))
    least = 1 if total - largest >= count - 1 else 0
    counts, surplus = [largest] + [least] * (count - 1), total - largest - least * (count - 1)
    while surplus > 0:
        free = [i for i in range(1, count) if counts[i] < largest] or [i for i in range(1, count) if counts[i] < bound]
        mass, remaining = sum([weights[i] for i in free]), surplus
        for i in free:
            more = min(bound - counts[i], max(1, remaining * weights[i] // mass), surplus)
            counts[i] = counts[i] + more
            surplus = surplus - more
    return np.array(counts)


def bell_draw(key, dims, scale, reach, pieces=(), kind=jnp.bfloat16):
    factor_of = shard_levels(key, dims, pieces, -0.22, 0.18) if pieces else 1.0
    array = jax.random.normal(key, dims, jnp.float32) * scale * factor_of
    return jnp.minimum(jnp.maximum(array, -reach), reach).astype(kind)


def setup_inputs(seed: int = 0) -> dict:
    arg_keys = jax.random.split(jax.random.key(seed), 12)
    route_ids_keys = jax.random.split(jax.random.fold_in(arg_keys[0], 1), TOKENS // TOK_DEV)
    route_ids_turns = jax.random.permutation(jax.random.fold_in(arg_keys[0], 3), TOKENS // TOK_DEV)
    route_ids = jax.vmap(lambda own, number: assign_block(jax.random.fold_in(arg_keys[0], 2), own, number, TOK_DEV, EXPERTS, 2, CAP, 2))(route_ids_keys, route_ids_turns).reshape((TOKENS, 2))
    route_weight = jnp.clip(0.2 + 0.6 * jax.random.uniform(arg_keys[1], (TOKENS, 2), jnp.float32) ** shard_levels(arg_keys[1], (TOKENS, 2), ((0, 32),), -0.2, 0.2), 0.2, 0.8)
    input_float = bell_draw(arg_keys[2], (TOKENS, D), 1.0, 6.0, ((0, 32),))
    input_quant = bell_draw(arg_keys[3], (TOKENS, D), 1.0, 6.0, ((0, 32),))
    keep_mask = touch_ends((jax.random.randint(arg_keys[4], (TOKENS, D), 0, 2) < 1).astype(jnp.int32), jax.random.fold_in(arg_keys[4], 1), 0, 1)
    grad_mixed = bell_draw(arg_keys[5], (TOKENS, D), 32.0, 192.0, ((0, 32),))
    gate_weight = bell_draw(arg_keys[6], (EXPERTS, D, FF), D ** -0.5, 0.09375, ((0, 4), (2, 8)))
    up_weight = bell_draw(arg_keys[7], (EXPERTS, D, FF), D ** -0.5, 0.09375, ((0, 4), (2, 8)))
    down_base = bell_draw(arg_keys[8], (EXPERTS, FF, D), FF ** -0.5, 0.0625, ((0, 4), (1, 8)))
    down_round = bell_draw(arg_keys[9], (EXPERTS, FF, D), 2.0, 8.0, ((0, 4), (1, 8)))
    down_step = jnp.clip(jnp.exp(math.log(0.04) - 2.30258502 * jax.random.uniform(arg_keys[10], (EXPERTS, D), jnp.float32) ** shard_levels(arg_keys[10], (EXPERTS, D), ((0, 4),), -0.2, 0.2)), 0.004, 0.04)
    return dict(route_ids=route_ids, route_weight=route_weight, input_float=input_float, input_quant=input_quant, keep_mask=keep_mask, grad_mixed=grad_mixed, gate_weight=gate_weight, up_weight=up_weight, down_base=down_base, down_round=down_round, down_step=down_step)


def slots_of(route_ids):
    groups = route_ids.shape[0] // TOK_DEV
    flat = route_ids.reshape(groups, TOK_DEV * 2)
    onehot = (flat[:, :, None] == jnp.arange(EXPERTS, dtype=jnp.int32)[None, None, :]).astype(jnp.int32)
    before = jnp.cumsum(onehot, axis=1) - onehot
    return jnp.sum(before * onehot, axis=2).reshape(route_ids.shape[0], 2).astype(jnp.int32)


def reference(route_ids, route_weight, input_float, input_quant, keep_mask, grad_mixed, gate_weight, up_weight, down_base, down_round, down_step):
    tokens = route_ids.shape[0]
    groups = tokens // TOK_DEV
    slot = slots_of(route_ids)
    x_in = jnp.where(keep_mask == 1, input_quant, input_float)
    group = (jnp.arange(tokens, dtype=jnp.int32) // TOK_DEV).astype(jnp.int32)
    position = (group[:, None] * CAP + slot).astype(jnp.int32)
    x_pair = jnp.broadcast_to(x_in[:, None, :], (tokens, 2, D))
    rows = jnp.zeros((EXPERTS, groups * CAP, D), jnp.bfloat16).at[route_ids, position].set(x_pair)
    weighted = (route_weight[:, :, None] * grad_mixed.astype(jnp.float32)[:, None, :]).astype(jnp.bfloat16)
    cot = jnp.zeros((EXPERTS, groups * CAP, D), jnp.bfloat16).at[route_ids, position].set(weighted)

    def one_expert(items):
        rows_e, cot_e, gate_e, up_e, base_e, round_e, step_e = items
        gate = jnp.dot(rows_e, gate_e, preferred_element_type=jnp.float32)
        up = jnp.dot(rows_e, up_e, preferred_element_type=jnp.float32)
        hidden = (jax.nn.silu(gate) * up).astype(jnp.bfloat16)
        soft = jax.nn.sigmoid(round_e.astype(jnp.float32))
        quant = (base_e.astype(jnp.float32) + step_e[None, :] * soft).astype(jnp.bfloat16)
        out = jnp.dot(hidden, quant, preferred_element_type=jnp.float32).astype(jnp.bfloat16)
        grad_w = lax.dot_general(hidden, cot_e, (((0,), (0,)), ((), ())), preferred_element_type=jnp.float32)
        return out, grad_w * step_e[None, :] * soft * (1.0 - soft)

    expert_out, round_grad = lax.map(one_expert, (rows, cot, gate_weight, up_weight, down_base, down_round, down_step))
    picked = expert_out[route_ids, position].astype(jnp.float32)
    mixed = jnp.sum(route_weight[:, :, None] * picked, axis=1).astype(jnp.bfloat16)
    return mixed, round_grad
```

```python
import functools

import jax
import jax.numpy as jnp
from jax import lax
from jax.experimental import pallas as pl
from jax.experimental.pallas import tpu as pltpu
from jax.sharding import PartitionSpec as P

MESH = pl.DeviceIdType.MESH
VMEM_LIMIT = 56 * 1024 * 1024
F32 = jnp.float32
BF16 = jnp.bfloat16


def dot(a, b, dims=((1,), (0,)), precision=None):
    return lax.dot_general(
        a, b, (dims, ((), ())), precision=precision, preferred_element_type=F32
    )


def placing_of(ids, weights, member, capacity, lanes):
    count = ids.shape[0]
    span = 4 * capacity
    column = lax.broadcasted_iota(jnp.int32, (count, lanes), 1)
    expert = column // span
    inside = column - expert * span
    group = inside // capacity
    slot = (inside - group * capacity).astype(F32)
    first = ids[:, 0:1] == expert
    second = ids[:, 1:2] == expert
    named = first.astype(F32) + second.astype(F32)
    earlier = lax.broadcasted_iota(jnp.int32, (count, count), 1) < lax.broadcasted_iota(
        jnp.int32, (count, count), 0
    )
    before = dot(earlier.astype(F32), named)
    here = (before == slot) & (group == member)
    placing = jnp.where(here, named, 0.0)
    weighting = jnp.where(here & first, weights[:, 0:1], 0.0) + jnp.where(
        here & second, weights[:, 1:2], 0.0
    )
    return placing, weighting


def stack_halves(rows):
    half = rows.shape[1] // 2
    return jnp.concatenate([rows[:, :half], rows[:, half:]], axis=0)


def layer_kernel(
    experts,
    reps,
    ids_ref,
    wts_ref,
    xf_ref,
    xq_ref,
    keep_ref,
    grad_ref,
    step_ref,
    gate_hbm,
    up_hbm,
    base_hbm,
    round_hbm,
    mixed_ref,
    hidden_ref,
    cot_hbm,
    wg,
    wu,
    quant,
    rounding,
    meta,
    xs,
    gs,
    xz,
    gz,
    xsend,
    gsend,
    xr,
    gr,
    gacc,
    uacc,
    osend,
    orecv,
    oacc,
    rs_send,
    rs_recv,
    ret_send,
    ret,
    load_sem,
    send_sem,
    recv_sem,
):
    me_e = lax.axis_index("expert")
    me_r = lax.axis_index("rep")
    core = lax.rem(me_r, 2)
    chip = me_r // 2
    chips = reps // 2
    pairs = chips // 2
    my_pair = chip // 2
    my_low = lax.rem(chip, 2)
    other_core = chip * 2 + 1 - core
    count, width = xf_ref.shape
    half = width // 2
    quarter = half // 2
    capacity = count // 2
    lanes = meta.shape[2]
    span = 4 * capacity
    hidden_width = wg.shape[1]
    counter = [0]

    def rep_at(offset):
        return lax.rem(me_r + offset, reps)

    def expert_at(offset):
        return lax.rem(me_e + offset, experts)

    def chip_at(j, i):
        return lax.rem(my_pair + j, pairs) * 2 + lax.rem(my_low + i, 2)

    def remote(source, target, expert, rep):
        index = counter[0]
        counter[0] += 1
        return pltpu.make_async_remote_copy(
            src_ref=source,
            dst_ref=target,
            send_sem=send_sem.at[index],
            recv_sem=recv_sem.at[index],
            device_id={"expert": expert, "rep": rep},
            device_id_type=MESH,
        )

    barrier = pltpu.get_barrier_semaphore()
    peers = [(me_e, rep_at(k)) for k in range(1, reps)]
    for k in range(1, experts):
        peers += [(expert_at(k), me_r), (expert_at(k), other_core)]
    for expert, rep in peers:
        pl.semaphore_signal(
            barrier, inc=1, device_id={"expert": expert, "rep": rep}, device_id_type=MESH
        )

    loads = [
        pltpu.make_async_copy(source.at[0], target, load_sem.at[n])
        for n, (source, target) in enumerate(
            [(round_hbm, rounding), (base_hbm, quant), (gate_hbm, wg), (up_hbm, wu)]
        )
    ]
    for load in loads:
        load.start()

    x_in = jnp.where(keep_ref[...] == 1, xq_ref[...].astype(F32), xf_ref[...].astype(F32))
    xs[core] = stack_halves(x_in).astype(BF16)
    gs[core] = stack_halves(grad_ref[...].astype(F32)).astype(BF16)
    ids = ids_ref[...]
    wts = wts_ref[...]
    placing, weighting = placing_of(ids, wts, lax.rem(me_r, 4), capacity, lanes)
    meta[me_r, 0:count, :] = placing
    meta[me_r, count : 2 * count, :] = weighting

    pl.semaphore_wait(barrier, len(peers))

    x_pair = remote(xs.at[core], xs.at[core], me_e, other_core)
    g_pair = remote(gs.at[core], gs.at[core], me_e, other_core)
    x_pair.start()
    g_pair.start()
    metas = [remote(meta.at[me_r], meta.at[me_r], me_e, rep_at(k)) for k in range(1, reps)]
    for copy in metas:
        copy.start()

    def quantise(start, stop):
        @pl.loop(start, stop)
        def _(n):
            rows = pl.ds(pl.multiple_of(n * 16, 16), 16)
            soft = jax.nn.sigmoid(rounding[rows, :].astype(F32))
            quant[rows, :] = (quant[rows, :].astype(F32) + step_ref[...] * soft).astype(BF16)

    def own_half(stacked):
        parts = []
        for c in range(2):
            both = stacked[c].astype(F32)
            parts.append(jnp.where(core == 0, both[:count], both[count:]))
        return jnp.concatenate(parts, axis=0).astype(BF16)

    chip_offsets = [(j, i) for j in range(pairs) for i in range(2) if (j, i) != (0, 0)]

    def to_chips(blocks):
        copies = {}
        for j, i in chip_offsets:
            copies[j, i] = remote(
                blocks.at[chip], blocks.at[chip], me_e, chip_at(j, i) * 2 + core
            )
            copies[j, i].start()
        return copies

    x_pair.wait_recv()
    xz[chip] = own_half(xs)
    x_chips = to_chips(xz)
    g_pair.wait_recv()
    gz[chip] = own_half(gs)
    g_chips = to_chips(gz)

    for copy in metas:
        copy.wait_recv()

    loads[0].wait()
    loads[1].wait()
    chunks = hidden_width // 16
    quantise(0, chunks // 4)

    def placings(pair):
        block = meta[pl.ds(pair * 4, 4)]
        place = block[:, 0:count, :].reshape(4 * count, lanes)
        weight = block[:, count:, :].reshape(4 * count, lanes)
        return place, weight

    def dispatch(j, blocks, copies, sent, received, weighted):
        for i in range(2):
            if (j, i) in copies:
                copies[j, i].wait_recv()
        pair = lax.rem(my_pair + pairs - j, pairs)
        place, weight = placings(pair)
        tokens = blocks[pl.ds(pair * 2, 2)].reshape(4 * count, half)
        picked = dot(place.astype(BF16), tokens, ((0,), (0,)))[: experts * span]
        if weighted:
            scale = dot(
                weight, jnp.ones((4 * count, 128), F32), ((0,), (0,)), lax.Precision.HIGHEST
            )
            picked = picked * scale[: experts * span, 0:1]
        sent[pair] = picked.astype(BF16).reshape(experts, span, half)
        flying = []
        for k in range(1, experts):
            expert = expert_at(k)
            copy = remote(
                sent.at[pair, expert], received.at[core, pair * experts + me_e], expert, me_r
            )
            copy.start()
            flying.append(copy)
        received[core, pair * experts + me_e] = sent[pair, me_e]
        return pair, flying

    def forward(pair, received):
        blocks = received.at[core, pl.ds(pair * experts, experts)]
        copy = remote(blocks, blocks, me_e, other_core)
        copy.start()
        return copy

    flights = []
    x_sent = []
    for j in range(pairs):
        x_sent.append(dispatch(j, xz, x_chips, xsend, xr, False))
        quantise(chunks * (1 + j) // (2 + pairs), chunks * (2 + j) // (2 + pairs))
    g_sent = [dispatch(j, gz, g_chips, gsend, gr, True) for j in range(pairs)]
    x_forward = []
    for pair, flying in x_sent:
        for copy in flying:
            copy.wait_recv()
        x_forward.append(forward(pair, xr))
    quantise(chunks * (1 + pairs) // (2 + pairs), chunks)

    loads[2].wait()
    loads[3].wait()
    gacc[...] = jnp.zeros_like(gacc)
    uacc[...] = jnp.zeros_like(uacc)
    depth = min(512, half)

    def gate_up(side):
        @pl.loop(0, half // depth)
        def _(k):
            columns = pl.ds(pl.multiple_of(k * depth, depth), depth)
            rows = pl.ds(pl.multiple_of(side * half + k * depth, depth), depth)
            block = xr[side, :, :, columns].reshape(-1, depth)
            gacc[...] += dot(block, wg[rows, :])
            uacc[...] += dot(block, wu[rows, :])

    gate_up(core)
    for copy in x_forward:
        copy.wait_recv()
    gate_up(1 - core)
    gate = gacc[...]
    hidden = (gate / (1.0 + jnp.exp(-gate)) * uacc[...]).astype(BF16)
    hidden_ref[...] = hidden

    g_forward = []
    for pair, flying in g_sent:
        for copy in flying:
            copy.wait_recv()
        g_forward.append(forward(pair, gr))

    def down(side, result):
        @pl.loop(0, half // depth)
        def _(k):
            columns = pl.ds(pl.multiple_of(k * depth, depth), depth)
            source = pl.ds(pl.multiple_of(side * half + k * depth, depth), depth)
            result[:, columns] = dot(hidden_ref[...], quant[:, source]).astype(result.dtype)

    down(1 - core, osend)
    o_pair = remote(osend, orecv, me_e, other_core)
    o_pair.start()
    down(core, oacc)
    for copy in g_forward:
        copy.wait_recv()
    cot_out = pltpu.make_async_copy(gr, cot_hbm, load_sem.at[4])
    cot_out.start()
    o_pair.wait_recv()
    for z in range(chips):
        rows = []
        for e in range(experts):
            start = (z // 2 * experts + e) * span + z % 2 * 2 * capacity
            part = oacc[start : start + 2 * capacity, :]
            block = start // span * span
            got = orecv[block : block + span, :].astype(F32)
            rows.append(part + got[start - block : start - block + 2 * capacity])
        rs_send[z] = jnp.concatenate(rows, axis=0).astype(BF16)
    rs_copies = []
    for n, (j, i) in enumerate(chip_offsets):
        there = chip_at(j, i)
        copy = remote(rs_send.at[there], rs_recv.at[n], me_e, there * 2 + core)
        copy.start()
        rs_copies.append(copy)
    total = rs_send[chip].astype(F32)
    for n, copy in enumerate(rs_copies):
        copy.wait_recv()
        total = total + rs_recv[n].astype(F32)
    for e in range(experts):
        part = total[e * 2 * capacity : (e + 1) * 2 * capacity]
        ret_send[e] = stack_halves(part).astype(BF16)
    ret_copies = []
    for k in range(experts):
        expert = expert_at(k)
        for rep in (me_r, other_core):
            if k == 0 and rep is me_r:
                continue
            copy = remote(ret_send.at[expert], ret.at[core, me_e], expert, rep)
            copy.start()
            ret_copies.append(copy)
    ret[core, me_e] = ret_send[me_e]
    weightings = [
        placing_of(ids, wts, 2 * q + core, capacity, lanes)[1][:, : experts * span]
        for q in range(2)
    ]
    for copy in ret_copies:
        copy.wait_recv()
    for h in range(2):
        rows = ret[h].astype(F32).reshape(experts * span, quarter)
        for q in range(2):
            start = h * half + q * quarter
            mixed_ref[:, start : start + quarter] = dot(
                weightings[q], rows, precision=lax.Precision.HIGHEST
            ).astype(BF16)

    cot_out.wait()
    sent = [x_pair, g_pair, o_pair] + metas + x_forward + g_forward + rs_copies + ret_copies
    sent += list(x_chips.values()) + list(g_chips.values())
    for _, flying in x_sent + g_sent:
        sent += flying
    for copy in sent:
        copy.wait_send()


def round_kernel(hidden_ref, cot_ref, round_ref, step_ref, out_ref):
    hidden = hidden_ref[...]
    half = cot_ref.shape[3]
    for h in range(2):
        columns = slice(h * half, (h + 1) * half)
        soft = jax.nn.sigmoid(round_ref[0, :, columns].astype(F32))
        grad = dot(hidden, cot_ref[h].reshape(-1, half), ((0,), (0,)))
        out_ref[0, :, columns] = grad * step_ref[:, columns] * soft * (1.0 - soft)


def fused_body(
    experts,
    reps,
    route_ids,
    route_weight,
    input_float,
    input_quant,
    keep_mask,
    grad_mixed,
    gate_weight,
    up_weight,
    down_base,
    down_round,
    down_step,
):
    count, width = input_float.shape
    half = width // 2
    hidden_width = gate_weight.shape[2]
    capacity = count // 2
    span = 4 * capacity
    chips = reps // 2
    pairs = chips // 2
    rows = reps * experts * capacity
    copies = 2 + (reps - 1) + 2 * (chips - 1) + 2 * pairs * (experts - 1)
    copies += 2 * pairs + 1 + (chips - 1) + 2 * experts
    vmem = pl.BlockSpec(memory_space=pltpu.VMEM)
    anywhere = pl.BlockSpec(memory_space=pl.ANY)
    mixed, hidden, cot = pl.pallas_call(
        functools.partial(layer_kernel, experts, reps),
        out_shape=(
            jax.ShapeDtypeStruct((count, width), BF16),
            jax.ShapeDtypeStruct((rows, hidden_width), BF16),
            jax.ShapeDtypeStruct((2, pairs * experts, span, half), BF16),
        ),
        in_specs=[vmem] * 7 + [anywhere] * 4,
        out_specs=(vmem, vmem, anywhere),
        scratch_shapes=[
            pltpu.VMEM((width, hidden_width), BF16),
            pltpu.VMEM((width, hidden_width), BF16),
            pltpu.VMEM((hidden_width, width), BF16),
            pltpu.VMEM((hidden_width, width), BF16),
            pltpu.VMEM((reps, 2 * count, 128), F32),
            pltpu.VMEM((2, 2 * count, half), BF16),
            pltpu.VMEM((2, 2 * count, half), BF16),
            pltpu.VMEM((chips, 2 * count, half), BF16),
            pltpu.VMEM((chips, 2 * count, half), BF16),
            pltpu.VMEM((pairs, experts, span, half), BF16),
            pltpu.VMEM((pairs, experts, span, half), BF16),
            pltpu.VMEM((2, pairs * experts, span, half), BF16),
            pltpu.VMEM((2, pairs * experts, span, half), BF16),
            pltpu.VMEM((rows, hidden_width), F32),
            pltpu.VMEM((rows, hidden_width), F32),
            pltpu.VMEM((rows, half), BF16),
            pltpu.VMEM((rows, half), BF16),
            pltpu.VMEM((rows, half), F32),
            pltpu.VMEM((chips, experts * 2 * capacity, half), BF16),
            pltpu.VMEM((chips - 1, experts * 2 * capacity, half), BF16),
            pltpu.VMEM((experts, span, half // 2), BF16),
            pltpu.VMEM((2, experts, span, half // 2), BF16),
            pltpu.SemaphoreType.DMA((5,)),
            pltpu.SemaphoreType.DMA((copies,)),
            pltpu.SemaphoreType.DMA((copies,)),
        ],
        compiler_params=pltpu.CompilerParams(
            collective_id=0, has_side_effects=True, vmem_limit_bytes=VMEM_LIMIT
        ),
        cost_estimate=pl.CostEstimate(
            flops=6 * rows * width * hidden_width,
            bytes_accessed=8 * width * hidden_width,
            transcendentals=width * hidden_width,
        ),
        name="layer",
    )(
        route_ids,
        route_weight,
        input_float,
        input_quant,
        keep_mask,
        grad_mixed,
        down_step,
        gate_weight,
        up_weight,
        down_base,
        down_round,
    )
    tile = 128
    round_grad = pl.pallas_call(
        round_kernel,
        out_shape=jax.ShapeDtypeStruct((1, hidden_width, width), F32),
        grid=(hidden_width // tile,),
        in_specs=[
            pl.BlockSpec((rows, tile), lambda n: (0, n)),
            pl.BlockSpec((2, pairs * experts, span, half), lambda n: (0, 0, 0, 0)),
            pl.BlockSpec((1, tile, width), lambda n: (0, n, 0)),
            pl.BlockSpec((1, width), lambda n: (0, 0)),
        ],
        out_specs=pl.BlockSpec((1, tile, width), lambda n: (0, n, 0)),
        compiler_params=pltpu.CompilerParams(vmem_limit_bytes=VMEM_LIMIT),
        cost_estimate=pl.CostEstimate(
            flops=2 * rows * width * hidden_width,
            bytes_accessed=6 * width * hidden_width,
            transcendentals=width * hidden_width,
        ),
        name="round_grad",
    )(hidden, cot, down_round, down_step)
    return (mixed, round_grad)


def local_slots(route_ids, experts):
    count = route_ids.shape[0]
    flat = route_ids.reshape(count * 2)
    onehot = (flat[:, None] == jnp.arange(experts, dtype=jnp.int32)[None, :]).astype(jnp.int32)
    before = jnp.cumsum(onehot, axis=0) - onehot
    return jnp.sum(before * onehot, axis=1).reshape(count, 2)


def body(
    route_ids,
    route_weight,
    input_float,
    input_quant,
    keep_mask,
    grad_mixed,
    gate_weight,
    up_weight,
    down_base,
    down_round,
    down_step,
):
    experts = lax.axis_size("expert")
    count = route_ids.shape[0]
    capacity = count // 2
    slot = local_slots(route_ids, experts)
    target = route_ids * capacity + slot
    columns = jnp.arange(experts * capacity, dtype=jnp.int32)
    first = (target[:, 0:1] == columns[None, :]).astype(jnp.float32)
    second = (target[:, 1:2] == columns[None, :]).astype(jnp.float32)
    placing = (first + second).astype(jnp.bfloat16)
    weighting = route_weight[:, 0:1] * first + route_weight[:, 1:2] * second
    x_in = jnp.where(keep_mask == 1, input_quant, input_float)
    send_rows = lax.dot_general(
        placing, x_in, (((0,), (0,)), ((), ())), preferred_element_type=jnp.float32
    ).astype(jnp.bfloat16)
    send_cot = lax.dot_general(
        weighting,
        grad_mixed.astype(jnp.float32),
        (((0,), (0,)), ((), ())),
        precision=lax.Precision.HIGHEST,
        preferred_element_type=jnp.float32,
    ).astype(jnp.bfloat16)
    own_rows, own_cot = (
        lax.all_to_all(send_rows, "expert", split_axis=0, concat_axis=0, tiled=True),
        lax.all_to_all(send_cot, "expert", split_axis=0, concat_axis=0, tiled=True),
    )
    w_gate = gate_weight[0]
    w_up = up_weight[0]
    soft = jax.nn.sigmoid(down_round[0].astype(jnp.float32))
    step_row = down_step[0][None, :]
    quant_down = (down_base[0].astype(jnp.float32) + step_row * soft).astype(jnp.bfloat16)
    all_rows, all_cot = (
        lax.all_gather(own_rows, "rep", axis=0, tiled=True),
        lax.all_gather(own_cot, "rep", axis=0, tiled=True),
    )
    gate = jnp.dot(all_rows, w_gate, preferred_element_type=jnp.float32)
    up = jnp.dot(all_rows, w_up, preferred_element_type=jnp.float32)
    hidden = (jax.nn.silu(gate) * up).astype(jnp.bfloat16)
    grad_w = lax.dot_general(
        hidden, all_cot, (((0,), (0,)), ((), ())), preferred_element_type=jnp.float32
    )
    summed = lax.psum_scatter(
        jnp.dot(hidden, quant_down, preferred_element_type=jnp.float32),
        "rep",
        scatter_dimension=0,
        tiled=True,
    ).astype(jnp.bfloat16)
    returned = lax.all_to_all(summed, "expert", split_axis=0, concat_axis=0, tiled=True)
    mixed = jnp.dot(
        weighting,
        returned.astype(jnp.float32),
        precision=lax.Precision.HIGHEST,
        preferred_element_type=jnp.float32,
    ).astype(jnp.bfloat16)
    round_grad = (grad_w * step_row * soft * (1.0 - soft))[None]
    return (mixed, round_grad)


def solution(mesh):
    experts, reps = mesh.shape["expert"], mesh.shape["rep"]

    def choose(*args):
        count, width = args[2].shape
        hidden_width = args[6].shape[2]
        capacity = count // 2
        rows = reps * experts * capacity
        weights = 8 * width * hidden_width
        buffers = rows * (8 * hidden_width + 26 * width)
        fits = weights + buffers <= VMEM_LIMIT * 7 // 8
        fits = fits and hidden_width % 128 == 0 and reps % 4 == 0
        fits = fits and count % 8 == 0 and experts * 4 * capacity <= 128
        if fits:
            return fused_body(experts, reps, *args)
        return body(*args)

    return jax.shard_map(
        choose,
        mesh=mesh,
        in_specs=(
            P(("expert", "rep"), None),
            P(("expert", "rep"), None),
            P(("expert", "rep"), None),
            P(("expert", "rep"), None),
            P(("expert", "rep"), None),
            P(("expert", "rep"), None),
            P("expert", None, "rep"),
            P("expert", None, "rep"),
            P("expert", "rep", None),
            P("expert", "rep", None),
            P("expert", None),
        ),
        out_specs=(P(("expert", "rep"), None), P("expert", "rep", None)),
        check_vma=False,
    )
```

```python
import functools

import jax
import jax.numpy as jnp
from jax import lax
from jax.experimental import pallas as pl
from jax.experimental.pallas import tpu as pltpu
from jax.sharding import PartitionSpec as P

MESH = pl.DeviceIdType.MESH
VMEM_LIMIT = 56 * 1024 * 1024
F32 = jnp.float32
BF16 = jnp.bfloat16


def dot(a, b, dims=((1,), (0,)), precision=None):
    return lax.dot_general(
        a, b, (dims, ((), ())), precision=precision, preferred_element_type=F32
    )


def placing_of(ids, weights, member, capacity, lanes):
    count = ids.shape[0]
    span = 4 * capacity
    column = lax.broadcasted_iota(jnp.int32, (count, lanes), 1)
    expert = column // span
    inside = column - expert * span
    group = inside // capacity
    slot = (inside - group * capacity).astype(F32)
    first = ids[:, 0:1] == expert
    second = ids[:, 1:2] == expert
    named = first.astype(F32) + second.astype(F32)
    earlier = lax.broadcasted_iota(jnp.int32, (count, count), 1) < lax.broadcasted_iota(
        jnp.int32, (count, count), 0
    )
    before = dot(earlier.astype(F32), named)
    here = (before == slot) & (group == member)
    placing = jnp.where(here, named, 0.0)
    weighting = jnp.where(here & first, weights[:, 0:1], 0.0) + jnp.where(
        here & second, weights[:, 1:2], 0.0
    )
    return placing, weighting


def stack_halves(rows):
    half = rows.shape[1] // 2
    return jnp.concatenate([rows[:, :half], rows[:, half:]], axis=0)


def layer_kernel(
    experts,
    reps,
    ids_ref,
    wts_ref,
    xf_ref,
    xq_ref,
    keep_ref,
    grad_ref,
    step_ref,
    gate_hbm,
    up_hbm,
    base_hbm,
    round_hbm,
    mixed_ref,
    hidden_ref,
    cot_hbm,
    slope_hbm,
    wg,
    wu,
    quant,
    rounding,
    meta,
    xs,
    gs,
    xz,
    gz,
    xsend,
    gsend,
    xr,
    gr,
    gacc,
    uacc,
    osend,
    orecv,
    oacc,
    ret_send,
    ret,
    mix_send,
    mix_recv,
    load_sem,
    send_sem,
    recv_sem,
):
    me_e = lax.axis_index("expert")
    me_r = lax.axis_index("rep")
    core = lax.rem(me_r, 2)
    chip = me_r // 2
    chips = reps // 2
    pairs = chips // 2
    my_pair = chip // 2
    my_low = lax.rem(chip, 2)
    other_core = chip * 2 + 1 - core
    count, width = xf_ref.shape
    half = width // 2
    quarter = half // 2
    capacity = count // 2
    lanes = meta.shape[2]
    span = 4 * capacity
    hidden_width = wg.shape[1]
    counter = [0]

    def rep_at(offset):
        return lax.rem(me_r + offset, reps)

    def expert_at(offset):
        return lax.rem(me_e + offset, experts)

    def chip_at(j, i):
        return lax.rem(my_pair + j, pairs) * 2 + lax.rem(my_low + i, 2)

    def remote(source, target, expert, rep):
        index = counter[0]
        counter[0] += 1
        return pltpu.make_async_remote_copy(
            src_ref=source,
            dst_ref=target,
            send_sem=send_sem.at[index],
            recv_sem=recv_sem.at[index],
            device_id={"expert": expert, "rep": rep},
            device_id_type=MESH,
        )

    barrier = pltpu.get_barrier_semaphore()
    peers = [(me_e, rep_at(k)) for k in range(1, reps)]
    peers += [(expert_at(k), me_r) for k in range(1, experts)]
    for expert, rep in peers:
        pl.semaphore_signal(
            barrier, inc=1, device_id={"expert": expert, "rep": rep}, device_id_type=MESH
        )

    loads = [
        pltpu.make_async_copy(source.at[0], target, load_sem.at[n])
        for n, (source, target) in enumerate(
            [(round_hbm, rounding), (base_hbm, quant), (gate_hbm, wg), (up_hbm, wu)]
        )
    ]
    loads[0].start()
    loads[1].start()

    x_in = jnp.where(keep_ref[...] == 1, xq_ref[...].astype(F32), xf_ref[...].astype(F32))
    xs[core] = stack_halves(x_in).astype(BF16)
    gs[core] = stack_halves(grad_ref[...].astype(F32)).astype(BF16)
    eye = (
        lax.broadcasted_iota(jnp.int32, (count, count), 0)
        == lax.broadcasted_iota(jnp.int32, (count, count), 1)
    ).astype(F32)
    across = ((1,), (1,))
    ids = dot(eye, ids_ref[...].astype(F32), across, lax.Precision.HIGHEST).astype(jnp.int32)
    wts = dot(eye, wts_ref[...], across, lax.Precision.HIGHEST)
    placing, weighting = placing_of(ids, wts, lax.rem(me_r, 4), capacity, lanes)
    meta[me_r, 0:count, :] = placing
    meta[me_r, count : 2 * count, :] = weighting

    pl.semaphore_wait(barrier, len(peers))

    x_pair = remote(xs.at[core], xs.at[core], me_e, other_core)
    g_pair = remote(gs.at[core], gs.at[core], me_e, other_core)
    x_pair.start()
    g_pair.start()
    metas = [remote(meta.at[me_r], meta.at[me_r], me_e, rep_at(k)) for k in range(1, reps)]
    for copy in metas:
        copy.start()

    def quantise(start, stop):
        @pl.loop(start, stop)
        def _(n):
            rows = pl.ds(pl.multiple_of(n * 16, 16), 16)
            soft = jax.nn.sigmoid(rounding[rows, :].astype(F32))
            scaled = step_ref[...] * soft
            quant[rows, :] = (quant[rows, :].astype(F32) + scaled).astype(BF16)
            rounding[rows, :] = (scaled * (1.0 - soft)).astype(BF16)

    def own_half(stacked):
        parts = []
        for c in range(2):
            both = stacked[c].astype(F32)
            parts.append(jnp.where(core == 0, both[:count], both[count:]))
        return jnp.concatenate(parts, axis=0).astype(BF16)

    chip_offsets = [(j, i) for j in range(pairs) for i in range(2) if (j, i) != (0, 0)]

    def to_chips(blocks):
        copies = {}
        for j, i in chip_offsets:
            copies[j, i] = remote(
                blocks.at[chip], blocks.at[chip], me_e, chip_at(j, i) * 2 + core
            )
            copies[j, i].start()
        return copies

    x_pair.wait_recv()
    xz[chip] = own_half(xs)
    x_chips = to_chips(xz)
    g_pair.wait_recv()
    gz[chip] = own_half(gs)

    for copy in metas:
        copy.wait_recv()

    loads[0].wait()
    loads[1].wait()
    loads[2].start()
    loads[3].start()
    chunks = hidden_width // 16
    quantise(0, chunks // 4)

    def placings(pair):
        block = meta[pl.ds(pair * 4, 4)]
        place = block[:, 0:count, :].reshape(4 * count, lanes)
        weight = block[:, count:, :].reshape(4 * count, lanes)
        return place, weight

    def dispatch(j, blocks, copies, sent, received, weighted):
        for i in range(2):
            if (j, i) in copies:
                copies[j, i].wait_recv()
        pair = lax.rem(my_pair + pairs - j, pairs)
        place, weight = placings(pair)
        tokens = blocks[pl.ds(pair * 2, 2)].reshape(4 * count, half)
        picked = dot(place.astype(BF16), tokens, ((0,), (0,)))[: experts * span]
        if weighted:
            scale = dot(
                weight, jnp.ones((4 * count, 128), F32), ((0,), (0,)), lax.Precision.HIGHEST
            )
            picked = picked * scale[: experts * span, 0:1]
        sent[pair] = picked.astype(BF16).reshape(experts, span, half)
        flying = []
        for k in range(1, experts):
            expert = expert_at(k)
            copy = remote(
                sent.at[pair, expert], received.at[core, pair * experts + me_e], expert, me_r
            )
            copy.start()
            flying.append(copy)
        received[core, pair * experts + me_e] = sent[pair, me_e]
        return pair, flying

    def forward(pair, received):
        blocks = received.at[core, pl.ds(pair * experts, experts)]
        copy = remote(blocks, blocks, me_e, other_core)
        copy.start()
        return copy

    x_sent = []
    for j in range(pairs):
        x_sent.append(dispatch(j, xz, x_chips, xsend, xr, False))
        if j == pairs - 1:
            g_chips = to_chips(gz)
        quantise(chunks * (1 + j) // (2 + pairs), chunks * (2 + j) // (2 + pairs))
    x_forward = []
    for pair, flying in x_sent:
        for copy in flying:
            copy.wait_recv()
        x_forward.append(forward(pair, xr))
    quantise(chunks * (1 + pairs) // (2 + pairs), chunks)
    slope_out = pltpu.make_async_copy(rounding, slope_hbm, load_sem.at[5])
    slope_out.start()
    g_sent = [dispatch(0, gz, g_chips, gsend, gr, True)]

    loads[2].wait()
    loads[3].wait()
    gacc[...] = jnp.zeros_like(gacc)
    uacc[...] = jnp.zeros_like(uacc)
    depth = min(512, half)

    def gate_up(side):
        @pl.loop(0, half // depth)
        def _(k):
            columns = pl.ds(pl.multiple_of(k * depth, depth), depth)
            rows = pl.ds(pl.multiple_of(side * half + k * depth, depth), depth)
            block = xr[side, :, :, columns].reshape(-1, depth)
            gacc[...] += dot(block, wg[rows, :])
            uacc[...] += dot(block, wu[rows, :])

    gate_up(core)
    g_sent += [dispatch(j, gz, g_chips, gsend, gr, True) for j in range(1, pairs)]
    for copy in x_forward:
        copy.wait_recv()
    gate_up(1 - core)
    gate = gacc[...]
    hidden = (gate / (1.0 + jnp.exp(-gate)) * uacc[...]).astype(BF16)
    hidden_ref[...] = hidden

    def down(side, result):
        @pl.loop(0, half // depth)
        def _(k):
            columns = pl.ds(pl.multiple_of(k * depth, depth), depth)
            source = pl.ds(pl.multiple_of(side * half + k * depth, depth), depth)
            result[:, columns] = dot(hidden_ref[...], quant[:, source]).astype(result.dtype)

    down(1 - core, osend)
    o_pair = remote(osend, orecv, me_e, other_core)
    o_pair.start()
    down(core, oacc)
    o_pair.wait_recv()
    returning = []
    for j in range(pairs):
        pair = lax.rem(my_pair + 1 + j, pairs)
        rows = pl.ds(pl.multiple_of(pair * experts * span, experts * span), experts * span)
        both = oacc[rows, :] + orecv[rows, :].astype(F32)
        ret_send[pair] = both.astype(BF16).reshape(experts, span, half)
        flying = []
        for k in range(1, experts):
            expert = expert_at(k)
            copy = remote(ret_send.at[pair, expert], ret.at[pair, me_e], expert, me_r)
            copy.start()
            flying.append(copy)
        ret[pair, me_e] = ret_send[pair, me_e]
        returning.append((pair, flying))
    g_forward = []
    for pair, flying in g_sent:
        for copy in flying:
            copy.wait_recv()
        g_forward.append(forward(pair, gr))
    member = lax.rem(me_r, 4)
    mix_copies = []
    for j, (pair, flying) in enumerate(returning):
        weight = placings(pair)[1][:, : experts * span]
        parts = []
        for _ in range(3):
            parts.append(weight.astype(BF16))
            weight = weight - parts[-1].astype(F32)
        for copy in flying:
            copy.wait_recv()
        mix = dot(jnp.concatenate(parts, axis=0), ret[pair].reshape(experts * span, half))
        mix = mix.reshape(3, 4 * count, half).sum(axis=0)
        for d in range(4):
            rows = mix[d * count : (d + 1) * count]
            mix_send[pair, d] = stack_halves(rows).astype(BF16)
        for i in range(4):
            if (j, i) == (pairs - 1, 0):
                mix_recv[me_r] = mix_send[my_pair, member]
                continue
            there = lax.rem(member + i, 4)
            copy = remote(mix_send.at[pair, there], mix_recv.at[me_r], me_e, pair * 4 + there)
            copy.start()
            mix_copies.append(copy)
    for copy in g_forward:
        copy.wait_recv()
    cot_out = pltpu.make_async_copy(gr, cot_hbm, load_sem.at[4])
    cot_out.start()
    for copy in mix_copies:
        copy.wait_recv()
    for h in range(2):
        total = mix_recv[h].astype(F32)
        for z in range(1, chips):
            total = total + mix_recv[2 * z + h].astype(F32)
        for q in range(2):
            start = h * half + q * quarter
            rows = total[q * count : (q + 1) * count]
            mixed_ref[:, start : start + quarter] = rows.astype(BF16)

    slope_out.wait()
    cot_out.wait()
    sent = [x_pair, g_pair, o_pair] + metas + x_forward + g_forward + mix_copies
    sent += list(x_chips.values()) + list(g_chips.values())
    for _, flying in x_sent + g_sent + returning:
        sent += flying
    for copy in sent:
        copy.wait_send()


def round_kernel(hidden_ref, cot_ref, slope_ref, out_ref):
    hidden = hidden_ref[...]
    half = cot_ref.shape[3]
    for h in range(2):
        columns = slice(h * half, (h + 1) * half)
        grad = dot(hidden, cot_ref[h].reshape(-1, half), ((0,), (0,)))
        out_ref[0, :, columns] = grad * slope_ref[:, columns].astype(F32)


def fused_body(
    experts,
    reps,
    route_ids,
    route_weight,
    input_float,
    input_quant,
    keep_mask,
    grad_mixed,
    gate_weight,
    up_weight,
    down_base,
    down_round,
    down_step,
):
    count, width = input_float.shape
    half = width // 2
    hidden_width = gate_weight.shape[2]
    capacity = count // 2
    span = 4 * capacity
    chips = reps // 2
    pairs = chips // 2
    rows = reps * experts * capacity
    copies = 2 + (reps - 1) + 2 * (chips - 1) + 2 * pairs * (experts - 1)
    copies += 2 * pairs + 1 + pairs * (experts - 1) + reps - 1
    vmem = pl.BlockSpec(memory_space=pltpu.VMEM)
    anywhere = pl.BlockSpec(memory_space=pl.ANY)
    mixed, hidden, cot, slope = pl.pallas_call(
        functools.partial(layer_kernel, experts, reps),
        out_shape=(
            jax.ShapeDtypeStruct((count, width), BF16),
            jax.ShapeDtypeStruct((rows, hidden_width), BF16),
            jax.ShapeDtypeStruct((2, pairs * experts, span, half), BF16),
            jax.ShapeDtypeStruct((hidden_width, width), BF16),
        ),
        in_specs=[vmem] * 7 + [anywhere] * 4,
        out_specs=(vmem, vmem, anywhere, anywhere),
        scratch_shapes=[
            pltpu.VMEM((width, hidden_width), BF16),
            pltpu.VMEM((width, hidden_width), BF16),
            pltpu.VMEM((hidden_width, width), BF16),
            pltpu.VMEM((hidden_width, width), BF16),
            pltpu.VMEM((reps, 2 * count, 128), F32),
            pltpu.VMEM((2, 2 * count, half), BF16),
            pltpu.VMEM((2, 2 * count, half), BF16),
            pltpu.VMEM((chips, 2 * count, half), BF16),
            pltpu.VMEM((chips, 2 * count, half), BF16),
            pltpu.VMEM((pairs, experts, span, half), BF16),
            pltpu.VMEM((pairs, experts, span, half), BF16),
            pltpu.VMEM((2, pairs * experts, span, half), BF16),
            pltpu.VMEM((2, pairs * experts, span, half), BF16),
            pltpu.VMEM((rows, hidden_width), F32),
            pltpu.VMEM((rows, hidden_width), F32),
            pltpu.VMEM((rows, half), BF16),
            pltpu.VMEM((rows, half), BF16),
            pltpu.VMEM((rows, half), F32),
            pltpu.VMEM((pairs, experts, span, half), BF16),
            pltpu.VMEM((pairs, experts, span, half), BF16),
            pltpu.VMEM((pairs, 4, 2 * count, half // 2), BF16),
            pltpu.VMEM((reps, 2 * count, half // 2), BF16),
            pltpu.SemaphoreType.DMA((6,)),
            pltpu.SemaphoreType.DMA((copies,)),
            pltpu.SemaphoreType.DMA((copies,)),
        ],
        compiler_params=pltpu.CompilerParams(
            collective_id=0, has_side_effects=True, vmem_limit_bytes=VMEM_LIMIT
        ),
        cost_estimate=pl.CostEstimate(
            flops=6 * rows * width * hidden_width,
            bytes_accessed=8 * width * hidden_width,
            transcendentals=width * hidden_width,
        ),
        name="layer",
    )(
        route_ids.T,
        route_weight.T,
        input_float,
        input_quant,
        keep_mask,
        grad_mixed,
        down_step,
        gate_weight,
        up_weight,
        down_base,
        down_round,
    )
    tile = 128
    round_grad = pl.pallas_call(
        round_kernel,
        out_shape=jax.ShapeDtypeStruct((1, hidden_width, width), F32),
        grid=(hidden_width // tile,),
        in_specs=[
            pl.BlockSpec((rows, tile), lambda n: (0, n)),
            pl.BlockSpec((2, pairs * experts, span, half), lambda n: (0, 0, 0, 0)),
            pl.BlockSpec((tile, width), lambda n: (n, 0)),
        ],
        out_specs=pl.BlockSpec((1, tile, width), lambda n: (0, n, 0)),
        compiler_params=pltpu.CompilerParams(vmem_limit_bytes=VMEM_LIMIT),
        cost_estimate=pl.CostEstimate(
            flops=2 * rows * width * hidden_width,
            bytes_accessed=6 * width * hidden_width,
            transcendentals=0,
        ),
        name="round_grad",
    )(hidden, cot, slope)
    return (mixed, round_grad)


def local_slots(route_ids, experts):
    count = route_ids.shape[0]
    flat = route_ids.reshape(count * 2)
    onehot = (flat[:, None] == jnp.arange(experts, dtype=jnp.int32)[None, :]).astype(jnp.int32)
    before = jnp.cumsum(onehot, axis=0) - onehot
    return jnp.sum(before * onehot, axis=1).reshape(count, 2)


def body(
    route_ids,
    route_weight,
    input_float,
    input_quant,
    keep_mask,
    grad_mixed,
    gate_weight,
    up_weight,
    down_base,
    down_round,
    down_step,
):
    experts = lax.axis_size("expert")
    count = route_ids.shape[0]
    capacity = count // 2
    slot = local_slots(route_ids, experts)
    target = route_ids * capacity + slot
    columns = jnp.arange(experts * capacity, dtype=jnp.int32)
    first = (target[:, 0:1] == columns[None, :]).astype(jnp.float32)
    second = (target[:, 1:2] == columns[None, :]).astype(jnp.float32)
    placing = (first + second).astype(jnp.bfloat16)
    weighting = route_weight[:, 0:1] * first + route_weight[:, 1:2] * second
    x_in = jnp.where(keep_mask == 1, input_quant, input_float)
    send_rows = lax.dot_general(
        placing, x_in, (((0,), (0,)), ((), ())), preferred_element_type=jnp.float32
    ).astype(jnp.bfloat16)
    send_cot = lax.dot_general(
        weighting,
        grad_mixed.astype(jnp.float32),
        (((0,), (0,)), ((), ())),
        precision=lax.Precision.HIGHEST,
        preferred_element_type=jnp.float32,
    ).astype(jnp.bfloat16)
    own_rows, own_cot = (
        lax.all_to_all(send_rows, "expert", split_axis=0, concat_axis=0, tiled=True),
        lax.all_to_all(send_cot, "expert", split_axis=0, concat_axis=0, tiled=True),
    )
    w_gate = gate_weight[0]
    w_up = up_weight[0]
    soft = jax.nn.sigmoid(down_round[0].astype(jnp.float32))
    step_row = down_step[0][None, :]
    quant_down = (down_base[0].astype(jnp.float32) + step_row * soft).astype(jnp.bfloat16)
    all_rows, all_cot = (
        lax.all_gather(own_rows, "rep", axis=0, tiled=True),
        lax.all_gather(own_cot, "rep", axis=0, tiled=True),
    )
    gate = jnp.dot(all_rows, w_gate, preferred_element_type=jnp.float32)
    up = jnp.dot(all_rows, w_up, preferred_element_type=jnp.float32)
    hidden = (jax.nn.silu(gate) * up).astype(jnp.bfloat16)
    grad_w = lax.dot_general(
        hidden, all_cot, (((0,), (0,)), ((), ())), preferred_element_type=jnp.float32
    )
    summed = lax.psum_scatter(
        jnp.dot(hidden, quant_down, preferred_element_type=jnp.float32),
        "rep",
        scatter_dimension=0,
        tiled=True,
    ).astype(jnp.bfloat16)
    returned = lax.all_to_all(summed, "expert", split_axis=0, concat_axis=0, tiled=True)
    mixed = jnp.dot(
        weighting,
        returned.astype(jnp.float32),
        precision=lax.Precision.HIGHEST,
        preferred_element_type=jnp.float32,
    ).astype(jnp.bfloat16)
    round_grad = (grad_w * step_row * soft * (1.0 - soft))[None]
    return (mixed, round_grad)


def solution(mesh):
    experts, reps = mesh.shape["expert"], mesh.shape["rep"]

    def choose(*args):
        count, width = args[2].shape
        hidden_width = args[6].shape[2]
        capacity = count // 2
        rows = reps * experts * capacity
        weights = 8 * width * hidden_width
        buffers = rows * (8 * hidden_width + 26 * width)
        fits = weights + buffers <= VMEM_LIMIT * 7 // 8
        fits = fits and hidden_width % 128 == 0 and reps % 4 == 0
        fits = fits and count % 8 == 0 and experts * 4 * capacity <= 128
        if fits:
            return fused_body(experts, reps, *args)
        return body(*args)

    return jax.shard_map(
        choose,
        mesh=mesh,
        in_specs=(
            P(("expert", "rep"), None),
            P(("expert", "rep"), None),
            P(("expert", "rep"), None),
            P(("expert", "rep"), None),
            P(("expert", "rep"), None),
            P(("expert", "rep"), None),
            P("expert", None, "rep"),
            P("expert", None, "rep"),
            P("expert", "rep", None),
            P("expert", "rep", None),
            P("expert", None),
        ),
        out_specs=(P(("expert", "rep"), None), P("expert", "rep", None)),
        check_vma=False,
    )
```

```python
import functools

import jax
import jax.numpy as jnp
from jax import lax
from jax.experimental import pallas as pl
from jax.experimental.pallas import tpu as pltpu
from jax.sharding import PartitionSpec as P

MESH = pl.DeviceIdType.MESH
VMEM_LIMIT = 56 * 1024 * 1024
F32 = jnp.float32
BF16 = jnp.bfloat16


def dot(a, b, dims=((1,), (0,)), precision=None):
    return lax.dot_general(
        a, b, (dims, ((), ())), precision=precision, preferred_element_type=F32
    )


def placing_of(ids, weights, member, capacity, lanes):
    count = ids.shape[0]
    span = 4 * capacity
    column = lax.broadcasted_iota(jnp.int32, (count, lanes), 1)
    expert = column // span
    inside = column - expert * span
    group = inside // capacity
    slot = (inside - group * capacity).astype(F32)
    first = ids[:, 0:1] == expert
    second = ids[:, 1:2] == expert
    named = first.astype(F32) + second.astype(F32)
    earlier = lax.broadcasted_iota(jnp.int32, (count, count), 1) < lax.broadcasted_iota(
        jnp.int32, (count, count), 0
    )
    before = dot(earlier.astype(F32), named)
    here = (before == slot) & (group == member)
    placing = jnp.where(here, named, 0.0)
    weighting = jnp.where(here & first, weights[:, 0:1], 0.0) + jnp.where(
        here & second, weights[:, 1:2], 0.0
    )
    return placing, weighting


def stack_halves(rows):
    half = rows.shape[1] // 2
    return jnp.concatenate([rows[:, :half], rows[:, half:]], axis=0)


def layer_kernel(
    experts,
    reps,
    ids_ref,
    wts_ref,
    xf_ref,
    xq_ref,
    keep_ref,
    grad_ref,
    step_ref,
    gate_hbm,
    up_hbm,
    base_hbm,
    round_hbm,
    mixed_ref,
    grad_hbm,
    hidden_ref,
    wg,
    wu,
    quant,
    rounding,
    meta,
    xs,
    gs,
    xz,
    gz,
    xsend,
    gsend,
    xr,
    gr,
    gacc,
    uacc,
    osend,
    orecv,
    oacc,
    ret_send,
    ret,
    mix_send,
    mix_recv,
    load_sem,
    send_sem,
    recv_sem,
):
    me_e = lax.axis_index("expert")
    me_r = lax.axis_index("rep")
    core = lax.rem(me_r, 2)
    chip = me_r // 2
    chips = reps // 2
    pairs = chips // 2
    my_pair = chip // 2
    my_low = lax.rem(chip, 2)
    other_core = chip * 2 + 1 - core
    count, width = xf_ref.shape
    half = width // 2
    quarter = half // 2
    capacity = count // 2
    lanes = meta.shape[2]
    span = 4 * capacity
    hidden_width = wg.shape[1]
    counter = [0]

    def rep_at(offset):
        return lax.rem(me_r + offset, reps)

    def expert_at(offset):
        return lax.rem(me_e + offset, experts)

    def chip_at(j, i):
        return lax.rem(my_pair + j, pairs) * 2 + lax.rem(my_low + i, 2)

    def remote(source, target, expert, rep):
        index = counter[0]
        counter[0] += 1
        return pltpu.make_async_remote_copy(
            src_ref=source,
            dst_ref=target,
            send_sem=send_sem.at[index],
            recv_sem=recv_sem.at[index],
            device_id={"expert": expert, "rep": rep},
            device_id_type=MESH,
        )

    barrier = pltpu.get_barrier_semaphore()
    peers = [(me_e, rep_at(k)) for k in range(1, reps)]
    peers += [(expert_at(k), me_r) for k in range(1, experts)]
    for expert, rep in peers:
        pl.semaphore_signal(
            barrier, inc=1, device_id={"expert": expert, "rep": rep}, device_id_type=MESH
        )

    loads = [
        pltpu.make_async_copy(source.at[0], target, load_sem.at[n])
        for n, (source, target) in enumerate(
            [(round_hbm, rounding), (base_hbm, quant), (gate_hbm, wg), (up_hbm, wu)]
        )
    ]
    loads[0].start()
    loads[1].start()

    x_in = jnp.where(keep_ref[...] == 1, xq_ref[...].astype(F32), xf_ref[...].astype(F32))
    xs[core] = stack_halves(x_in).astype(BF16)
    gs[core] = stack_halves(grad_ref[...].astype(F32)).astype(BF16)
    eye = (
        lax.broadcasted_iota(jnp.int32, (count, count), 0)
        == lax.broadcasted_iota(jnp.int32, (count, count), 1)
    ).astype(F32)
    across = ((1,), (1,))
    ids = dot(eye, ids_ref[...].astype(F32), across, lax.Precision.HIGHEST).astype(jnp.int32)
    wts = dot(eye, wts_ref[...], across, lax.Precision.HIGHEST)
    placing, weighting = placing_of(ids, wts, lax.rem(me_r, 4), capacity, lanes)
    meta[me_r, 0:count, :] = placing
    meta[me_r, count : 2 * count, :] = weighting

    pl.semaphore_wait(barrier, len(peers))

    x_pair = remote(xs.at[core], xs.at[core], me_e, other_core)
    g_pair = remote(gs.at[core], gs.at[core], me_e, other_core)
    x_pair.start()
    g_pair.start()
    metas = [remote(meta.at[me_r], meta.at[me_r], me_e, rep_at(k)) for k in range(1, reps)]
    for copy in metas:
        copy.start()

    def quantise(start, stop):
        @pl.loop(start, stop)
        def _(n):
            rows = pl.ds(pl.multiple_of(n * 16, 16), 16)
            t = jnp.tanh(0.5 * rounding[rows, :].astype(F32))
            step = 0.5 * step_ref[...]
            quant[rows, :] = (quant[rows, :].astype(F32) + (step + step * t)).astype(BF16)
            rounding[rows, :] = (0.5 * step * (1.0 - t * t)).astype(BF16)

    def own_half(stacked):
        parts = []
        for c in range(2):
            both = stacked[c].astype(F32)
            parts.append(jnp.where(core == 0, both[:count], both[count:]))
        return jnp.concatenate(parts, axis=0).astype(BF16)

    chip_offsets = [(j, i) for j in range(pairs) for i in range(2) if (j, i) != (0, 0)]

    def to_chips(blocks):
        copies = {}
        for j, i in chip_offsets:
            copies[j, i] = remote(
                blocks.at[chip], blocks.at[chip], me_e, chip_at(j, i) * 2 + core
            )
            copies[j, i].start()
        return copies

    x_pair.wait_recv()
    xz[chip] = own_half(xs)
    x_chips = to_chips(xz)
    g_pair.wait_recv()
    gz[chip] = own_half(gs)

    for copy in metas:
        copy.wait_recv()

    loads[0].wait()
    loads[1].wait()
    loads[2].start()
    loads[3].start()
    chunks = hidden_width // 16
    quantise(0, chunks // 4)

    def placings(pair):
        block = meta[pl.ds(pair * 4, 4)]
        place = block[:, 0:count, :].reshape(4 * count, lanes)
        weight = block[:, count:, :].reshape(4 * count, lanes)
        return place, weight

    def dispatch(j, blocks, copies, sent, received, weighted):
        for i in range(2):
            if (j, i) in copies:
                copies[j, i].wait_recv()
        pair = lax.rem(my_pair + pairs - j, pairs)
        place, weight = placings(pair)
        tokens = blocks[pl.ds(pair * 2, 2)].reshape(4 * count, half)
        picked = dot(place.astype(BF16), tokens, ((0,), (0,)))[: experts * span]
        if weighted:
            scale = dot(
                weight, jnp.ones((4 * count, 128), F32), ((0,), (0,)), lax.Precision.HIGHEST
            )
            picked = picked * scale[: experts * span, 0:1]
        sent[pair] = picked.astype(BF16).reshape(experts, span, half)
        flying = []
        for k in range(1, experts):
            expert = expert_at(k)
            copy = remote(
                sent.at[pair, expert], received.at[core, pair * experts + me_e], expert, me_r
            )
            copy.start()
            flying.append(copy)
        received[core, pair * experts + me_e] = sent[pair, me_e]
        return pair, flying

    def forward(pair, received):
        blocks = received.at[core, pl.ds(pair * experts, experts)]
        copy = remote(blocks, blocks, me_e, other_core)
        copy.start()
        return copy

    x_sent = []
    for j in range(pairs):
        x_sent.append(dispatch(j, xz, x_chips, xsend, xr, False))
        if j == pairs - 1:
            g_chips = to_chips(gz)
        quantise(chunks * (1 + j) // (2 + pairs), chunks * (2 + j) // (2 + pairs))
    x_forward = []
    for pair, flying in x_sent:
        for copy in flying:
            copy.wait_recv()
        x_forward.append(forward(pair, xr))
    quantise(chunks * (1 + pairs) // (2 + pairs), chunks)
    g_sent = [dispatch(0, gz, g_chips, gsend, gr, True)]

    loads[2].wait()
    loads[3].wait()
    gacc[...] = jnp.zeros_like(gacc)
    uacc[...] = jnp.zeros_like(uacc)
    depth = min(512, half)

    def gate_up(side):
        @pl.loop(0, half // depth)
        def _(k):
            columns = pl.ds(pl.multiple_of(k * depth, depth), depth)
            rows = pl.ds(pl.multiple_of(side * half + k * depth, depth), depth)
            block = xr[side, :, :, columns].reshape(-1, depth)
            gacc[...] += dot(block, wg[rows, :])
            uacc[...] += dot(block, wu[rows, :])

    gate_up(core)
    g_sent += [dispatch(j, gz, g_chips, gsend, gr, True) for j in range(1, pairs)]
    for copy in x_forward:
        copy.wait_recv()
    gate_up(1 - core)
    gate = gacc[...]
    hidden = (gate / (1.0 + jnp.exp(-gate)) * uacc[...]).astype(BF16)
    hidden_ref[...] = hidden

    def down(side, result):
        @pl.loop(0, half // depth)
        def _(k):
            columns = pl.ds(pl.multiple_of(k * depth, depth), depth)
            source = pl.ds(pl.multiple_of(side * half + k * depth, depth), depth)
            result[:, columns] = dot(hidden_ref[...], quant[:, source]).astype(result.dtype)

    down(1 - core, osend)
    o_pair = remote(osend, orecv, me_e, other_core)
    o_pair.start()
    down(core, oacc)
    o_pair.wait_recv()
    returning = []
    for j in range(pairs):
        pair = lax.rem(my_pair + 1 + j, pairs)
        rows = pl.ds(pl.multiple_of(pair * experts * span, experts * span), experts * span)
        both = oacc[rows, :] + orecv[rows, :].astype(F32)
        ret_send[pair] = both.astype(BF16).reshape(experts, span, half)
        flying = []
        for k in range(1, experts):
            expert = expert_at(k)
            copy = remote(ret_send.at[pair, expert], ret.at[pair, me_e], expert, me_r)
            copy.start()
            flying.append(copy)
        ret[pair, me_e] = ret_send[pair, me_e]
        returning.append((pair, flying))
    g_forward = []
    for pair, flying in g_sent:
        for copy in flying:
            copy.wait_recv()
        g_forward.append(forward(pair, gr))
    for copy in g_forward:
        copy.wait_recv()
    tile = 128
    tiles = hidden_width // tile
    grad_out = []

    def round_grad(start, stop):
        @pl.loop(start, stop)
        def _(n):
            rows = pl.ds(pl.multiple_of(n * tile, tile), tile)
            for h in range(2):
                columns = slice(h * half, (h + 1) * half)
                grad = dot(hidden_ref[:, rows], gr[h].reshape(-1, half), ((0,), (0,)))
                rounding[rows, columns] = (grad * rounding[rows, columns].astype(F32)).astype(BF16)

        span_rows = pl.ds(start * tile, (stop - start) * tile)
        copy = pltpu.make_async_copy(
            rounding.at[span_rows], grad_hbm.at[span_rows], load_sem.at[4 + len(grad_out)]
        )
        copy.start()
        grad_out.append(copy)

    round_grad(0, tiles // 2)
    member = lax.rem(me_r, 4)
    mix_copies = []
    for j, (pair, flying) in enumerate(returning):
        weight = placings(pair)[1][:, : experts * span]
        parts = []
        for _ in range(3):
            parts.append(weight.astype(BF16))
            weight = weight - parts[-1].astype(F32)
        for copy in flying:
            copy.wait_recv()
        mix = dot(jnp.concatenate(parts, axis=0), ret[pair].reshape(experts * span, half))
        mix = mix.reshape(3, 4 * count, half).sum(axis=0)
        for d in range(4):
            rows = mix[d * count : (d + 1) * count]
            mix_send[pair, d] = stack_halves(rows).astype(BF16)
        for i in range(4):
            if (j, i) == (pairs - 1, 0):
                mix_recv[me_r] = mix_send[my_pair, member]
                continue
            there = lax.rem(member + i, 4)
            copy = remote(mix_send.at[pair, there], mix_recv.at[me_r], me_e, pair * 4 + there)
            copy.start()
            mix_copies.append(copy)
    round_grad(tiles // 2, tiles)
    for copy in mix_copies:
        copy.wait_recv()
    for h in range(2):
        total = mix_recv[h].astype(F32)
        for z in range(1, chips):
            total = total + mix_recv[2 * z + h].astype(F32)
        for q in range(2):
            start = h * half + q * quarter
            rows = total[q * count : (q + 1) * count]
            mixed_ref[:, start : start + quarter] = rows.astype(BF16)

    for copy in grad_out:
        copy.wait()
    sent = [x_pair, g_pair, o_pair] + metas + x_forward + g_forward + mix_copies
    sent += list(x_chips.values()) + list(g_chips.values())
    for _, flying in x_sent + g_sent + returning:
        sent += flying
    for copy in sent:
        copy.wait_send()


def fused_body(
    experts,
    reps,
    route_ids,
    route_weight,
    input_float,
    input_quant,
    keep_mask,
    grad_mixed,
    gate_weight,
    up_weight,
    down_base,
    down_round,
    down_step,
):
    count, width = input_float.shape
    half = width // 2
    hidden_width = gate_weight.shape[2]
    capacity = count // 2
    span = 4 * capacity
    chips = reps // 2
    pairs = chips // 2
    rows = reps * experts * capacity
    copies = 2 + (reps - 1) + 2 * (chips - 1) + 2 * pairs * (experts - 1)
    copies += 2 * pairs + 1 + pairs * (experts - 1) + reps - 1
    vmem = pl.BlockSpec(memory_space=pltpu.VMEM)
    anywhere = pl.BlockSpec(memory_space=pl.ANY)
    mixed, grad = pl.pallas_call(
        functools.partial(layer_kernel, experts, reps),
        out_shape=(
            jax.ShapeDtypeStruct((count, width), BF16),
            jax.ShapeDtypeStruct((hidden_width, width), BF16),
        ),
        in_specs=[vmem] * 7 + [anywhere] * 4,
        out_specs=(vmem, anywhere),
        scratch_shapes=[
            pltpu.VMEM((rows, hidden_width), BF16),
            pltpu.VMEM((width, hidden_width), BF16),
            pltpu.VMEM((width, hidden_width), BF16),
            pltpu.VMEM((hidden_width, width), BF16),
            pltpu.VMEM((hidden_width, width), BF16),
            pltpu.VMEM((reps, 2 * count, 128), F32),
            pltpu.VMEM((2, 2 * count, half), BF16),
            pltpu.VMEM((2, 2 * count, half), BF16),
            pltpu.VMEM((chips, 2 * count, half), BF16),
            pltpu.VMEM((chips, 2 * count, half), BF16),
            pltpu.VMEM((pairs, experts, span, half), BF16),
            pltpu.VMEM((pairs, experts, span, half), BF16),
            pltpu.VMEM((2, pairs * experts, span, half), BF16),
            pltpu.VMEM((2, pairs * experts, span, half), BF16),
            pltpu.VMEM((rows, hidden_width), F32),
            pltpu.VMEM((rows, hidden_width), F32),
            pltpu.VMEM((rows, half), BF16),
            pltpu.VMEM((rows, half), BF16),
            pltpu.VMEM((rows, half), F32),
            pltpu.VMEM((pairs, experts, span, half), BF16),
            pltpu.VMEM((pairs, experts, span, half), BF16),
            pltpu.VMEM((pairs, 4, 2 * count, half // 2), BF16),
            pltpu.VMEM((reps, 2 * count, half // 2), BF16),
            pltpu.SemaphoreType.DMA((6,)),
            pltpu.SemaphoreType.DMA((copies,)),
            pltpu.SemaphoreType.DMA((copies,)),
        ],
        compiler_params=pltpu.CompilerParams(
            collective_id=0, has_side_effects=True, vmem_limit_bytes=VMEM_LIMIT
        ),
        cost_estimate=pl.CostEstimate(
            flops=8 * rows * width * hidden_width,
            bytes_accessed=8 * width * hidden_width,
            transcendentals=width * hidden_width,
        ),
        name="layer",
    )(
        route_ids.T,
        route_weight.T,
        input_float,
        input_quant,
        keep_mask,
        grad_mixed,
        down_step,
        gate_weight,
        up_weight,
        down_base,
        down_round,
    )
    return (mixed, grad.astype(F32)[None])


def local_slots(route_ids, experts):
    count = route_ids.shape[0]
    flat = route_ids.reshape(count * 2)
    onehot = (flat[:, None] == jnp.arange(experts, dtype=jnp.int32)[None, :]).astype(jnp.int32)
    before = jnp.cumsum(onehot, axis=0) - onehot
    return jnp.sum(before * onehot, axis=1).reshape(count, 2)


def body(
    route_ids,
    route_weight,
    input_float,
    input_quant,
    keep_mask,
    grad_mixed,
    gate_weight,
    up_weight,
    down_base,
    down_round,
    down_step,
):
    experts = lax.axis_size("expert")
    count = route_ids.shape[0]
    capacity = count // 2
    slot = local_slots(route_ids, experts)
    target = route_ids * capacity + slot
    columns = jnp.arange(experts * capacity, dtype=jnp.int32)
    first = (target[:, 0:1] == columns[None, :]).astype(jnp.float32)
    second = (target[:, 1:2] == columns[None, :]).astype(jnp.float32)
    placing = (first + second).astype(jnp.bfloat16)
    weighting = route_weight[:, 0:1] * first + route_weight[:, 1:2] * second
    x_in = jnp.where(keep_mask == 1, input_quant, input_float)
    send_rows = lax.dot_general(
        placing, x_in, (((0,), (0,)), ((), ())), preferred_element_type=jnp.float32
    ).astype(jnp.bfloat16)
    send_cot = lax.dot_general(
        weighting,
        grad_mixed.astype(jnp.float32),
        (((0,), (0,)), ((), ())),
        precision=lax.Precision.HIGHEST,
        preferred_element_type=jnp.float32,
    ).astype(jnp.bfloat16)
    own_rows, own_cot = (
        lax.all_to_all(send_rows, "expert", split_axis=0, concat_axis=0, tiled=True),
        lax.all_to_all(send_cot, "expert", split_axis=0, concat_axis=0, tiled=True),
    )
    w_gate = gate_weight[0]
    w_up = up_weight[0]
    soft = jax.nn.sigmoid(down_round[0].astype(jnp.float32))
    step_row = down_step[0][None, :]
    quant_down = (down_base[0].astype(jnp.float32) + step_row * soft).astype(jnp.bfloat16)
    all_rows, all_cot = (
        lax.all_gather(own_rows, "rep", axis=0, tiled=True),
        lax.all_gather(own_cot, "rep", axis=0, tiled=True),
    )
    gate = jnp.dot(all_rows, w_gate, preferred_element_type=jnp.float32)
    up = jnp.dot(all_rows, w_up, preferred_element_type=jnp.float32)
    hidden = (jax.nn.silu(gate) * up).astype(jnp.bfloat16)
    grad_w = lax.dot_general(
        hidden, all_cot, (((0,), (0,)), ((), ())), preferred_element_type=jnp.float32
    )
    summed = lax.psum_scatter(
        jnp.dot(hidden, quant_down, preferred_element_type=jnp.float32),
        "rep",
        scatter_dimension=0,
        tiled=True,
    ).astype(jnp.bfloat16)
    returned = lax.all_to_all(summed, "expert", split_axis=0, concat_axis=0, tiled=True)
    mixed = jnp.dot(
        weighting,
        returned.astype(jnp.float32),
        precision=lax.Precision.HIGHEST,
        preferred_element_type=jnp.float32,
    ).astype(jnp.bfloat16)
    round_grad = (grad_w * step_row * soft * (1.0 - soft))[None]
    return (mixed, round_grad)


def solution(mesh):
    experts, reps = mesh.shape["expert"], mesh.shape["rep"]

    def choose(*args):
        count, width = args[2].shape
        hidden_width = args[6].shape[2]
        capacity = count // 2
        rows = reps * experts * capacity
        weights = 8 * width * hidden_width
        buffers = rows * (8 * hidden_width + 26 * width)
        fits = weights + buffers <= VMEM_LIMIT * 7 // 8
        fits = fits and hidden_width % 128 == 0 and reps % 4 == 0
        fits = fits and count % 8 == 0 and experts * 4 * capacity <= 128
        if fits:
            return fused_body(experts, reps, *args)
        return body(*args)

    return jax.shard_map(
        choose,
        mesh=mesh,
        in_specs=(
            P(("expert", "rep"), None),
            P(("expert", "rep"), None),
            P(("expert", "rep"), None),
            P(("expert", "rep"), None),
            P(("expert", "rep"), None),
            P(("expert", "rep"), None),
            P("expert", None, "rep"),
            P("expert", None, "rep"),
            P("expert", "rep", None),
            P("expert", "rep", None),
            P("expert", None),
        ),
        out_specs=(P(("expert", "rep"), None), P("expert", "rep", None)),
        check_vma=False,
    )
```
